768 devices in a mesh: fsdp: 32 (over y, x), rep: 24 (over z, core).
Axes of the slice: x: 4, y: 8, z: 12, core: 2. Of those that a mesh axis runs over, the one named last changes fastest.
Arguments:
- local_weights: bfloat16 [24, 6144, 8192], P('rep', 'fsdp'), may hold values from -64 to 64
- base_weights: bfloat16 [6144, 8192], P('fsdp'), may hold values from -6 to 6
- momentum: float32 [6144, 8192], P(('fsdp', 'rep')), may hold values from -6 to 6
Outputs:
- new_weights: bfloat16 [6144, 8192], P('fsdp')
- new_momentum: float32 [6144, 8192], P(('fsdp', 'rep'))
The draws below stay inside these ranges and needn't reach their ends.
All inputs are finite; a program needn't handle non-finite values.
Results may differ from the reference program's by a relative error of at most 0.017.
Values may be sent and summed in bfloat16 or wider, within the bound.
No kernel may reach another device: no remote copies, remote signals or barrier semaphores. Data moves between devices by JAX's collectives and lax.ppermute only.
A program may use at most 64 MiB of HBM per device.

```python
import math
import jax
import jax.numpy as jnp
import numpy as np
from jax import lax

D = 8192
ROWS = 6144
N_REP = 24


def shared_layout(key):
    mask_key, low_key, level_key, side_key, power_key, free_key = jax.random.split(key, 6)
    common = jax.random.randint(mask_key, (ROWS, D), 0, 2) == 1
    low = jax.random.randint(low_key, (ROWS, D), -64, 65).astype(jnp.float32) / 32.0
    level = jax.random.randint(level_key, (ROWS, D), -7, 8).astype(jnp.float32)
    side = (2 * jax.random.randint(side_key, (ROWS, D), 0, 2) - 1).astype(jnp.float32)
    power = jax.random.randint(power_key, (ROWS, D // 128, 1), 0, 2)
    top_group = jnp.where(power == 1, 32.0, 16.0).astype(jnp.float32)
    top = jnp.broadcast_to(top_group, (ROWS, D // 128, 128)).reshape(ROWS, D)
    offset = (level + 0.375 * side) * top / 64.0
    noise = jax.random.normal(free_key, (ROWS, D), jnp.float32)
    free = jnp.clip(noise, -4.0, 4.0).astype(jnp.bfloat16).astype(jnp.float32)
    base = jnp.where(common, low + offset, free)
    return (base, common, low, top_group)


def draw_base_weights(key, part):
    base, common, low, top_group = shared_layout(key)
    return base.astype(jnp.bfloat16)


def draw_local_weights(key, part):
    common_share = 0.6
    own_share = 0.6
    base, common, low, top_group = shared_layout(key)
    key = jax.random.fold_in(key, 7)
    row_key, column_key, common_key, own_key = jax.random.split(key, 4)
    row_scale = jnp.exp(jax.random.uniform(row_key, (ROWS, 1), jnp.float32, math.log(0.3), math.log(3.0)))
    column_scale = jnp.exp(jax.random.uniform(column_key, (1, D), jnp.float32, math.log(0.3), math.log(3.0)))
    shared_noise = jnp.clip(jax.random.normal(common_key, (ROWS, D), jnp.float32), -4.0, 4.0)
    position = (jnp.arange(D, dtype=jnp.int32) % 128).reshape(1, D // 128, 128)

    def one_replica(index):
        replica_key = jax.random.fold_in(own_key, index)
        noise_key, spot_key, size_key, sign_key = jax.random.split(replica_key, 4)
        own = jnp.clip(jax.random.normal(noise_key, (ROWS, D), jnp.float32), -4.0, 4.0)
        delta = 0.3 * row_scale * column_scale * (common_share * shared_noise + own_share * own)
        spot = jax.random.randint(spot_key, (ROWS, D // 128, 1), 0, 128)
        spike_mask = (position == spot).reshape(ROWS, D)
        size = jax.random.uniform(size_key, (ROWS, D // 128, 1), jnp.float32, 1.05, 1.8)
        sign = (2 * jax.random.randint(sign_key, (ROWS, D // 128, 1), 0, 2) - 1).astype(jnp.float32)
        spike = jnp.broadcast_to(sign * size * top_group, (ROWS, D // 128, 128)).reshape(ROWS, D)
        local = jnp.where(spike_mask, base - spike, jnp.where(common, low, base - delta))
        return local.astype(jnp.bfloat16)
    return lax.map(one_replica, jnp.arange(N_REP, dtype=jnp.int32))


def shard_levels(key, shape, cuts, smallest, high):
    gain, own = 1.0, jax.random.fold_in(key, 6)
    for dim, blocks in cuts:
        steps = jnp.exp(jax.random.uniform(jax.random.fold_in(own, dim), (blocks,), jnp.float32, smallest / len(cuts), high / len(cuts)))
        gain = gain * jnp.repeat(steps, shape[dim] // blocks).reshape([-1 if axis == dim else 1 for axis in range(len(shape))])
    return gain


def scatter_about(rng, extent, deviation, most, shards=(), held_as=jnp.bfloat16):
    gain = shard_levels(rng, extent, shards, -0.22, 0.18) if shards else 1.0
    result = jax.random.normal(rng, extent, jnp.float32) * deviation * gain
    return jnp.minimum(jnp.maximum(result, -most), most).astype(held_as)


def setup_inputs(seed: int = 0) -> dict:
    key_list = jax.random.split(jax.random.key(seed), 4)
    return {
        "local_weights": draw_local_weights(jax.random.fold_in(key_list[3], 71), 0),
        "base_weights": draw_base_weights(jax.random.fold_in(key_list[3], 71), 0),
        "momentum": scatter_about(key_list[2], (ROWS, D), 1.0, 6.0, ((0, 768),), jnp.float32),
    }


EPSILON = 1e-6
TWO_POWERS = 2.0 ** np.arange(-24, 9)


def encode_levels(values):
    grouped = values.reshape(values.shape[:-1] + (values.shape[-1] // 128, 128))
    largest = jnp.max(jnp.abs(grouped), axis=-1)
    powers = jnp.asarray(TWO_POWERS, jnp.float32)
    scaling = jnp.min(jnp.where(powers >= largest[..., None], powers, powers[-1]), axis=-1)
    stretched = grouped * (128.0 / scaling)[..., None]
    lower = jnp.floor(stretched)
    codes = lower + jnp.where(stretched - lower >= 0.5, 1.0, 0.0)
    codes = jnp.clip(codes, -127.0, 127.0)
    return codes.astype(jnp.bfloat16).reshape(values.shape), scaling.astype(jnp.bfloat16)


def decode_levels(codes, scaling):
    grouped = codes.astype(jnp.float32).reshape(scaling.shape + (128,))
    return (grouped * (scaling.astype(jnp.float32) / 128.0)[..., None]).reshape(codes.shape)


def encode(values):
    grouped = values.reshape(values.shape[:-1] + (values.shape[-1] // 128, 128))
    largest = jnp.max(jnp.abs(grouped), axis=-1) + EPSILON
    scaling = largest.astype(jnp.bfloat16)
    encoded = (grouped / scaling.astype(jnp.float32)[..., None]).astype(jnp.bfloat16)
    return encoded.reshape(values.shape), scaling


def decode(encoded, scaling):
    grouped = encoded.astype(jnp.float32).reshape(scaling.shape + (128,))
    return (grouped * scaling.astype(jnp.float32)[..., None]).reshape(encoded.shape)


def reference(local_weights, base_weights, momentum):
    base_float = base_weights.astype(jnp.float32)

    def accumulate(carry, replica):
        codes, scaling = encode_levels(base_float - replica.astype(jnp.float32))
        return carry + decode_levels(codes, scaling), None

    summed, unused = lax.scan(accumulate, jnp.zeros(base_float.shape, jnp.float32), local_weights)
    average = summed / N_REP
    new_momentum = 0.9 * momentum + average
    outer = -0.7 * (average + 0.9 * new_momentum)
    encoded, scaling = encode(outer)
    new_weights = (base_float + decode(encoded, scaling)).astype(jnp.bfloat16)
    return new_weights, new_momentum
```

```python
import functools
import jax
import jax.numpy as jnp
from jax import lax
from jax.experimental import pallas as pl
from jax.experimental.pallas import tpu as pltpu
from jax.sharding import Mesh, PartitionSpec as P

EPSILON = 1e-06
GROUP = 128
BOTH = ("z", "core")
RIGHT = (1, 4, -2, 7)
LEFT = (-1, 2, -4, 5)
OWN = (0, 3, -3, 6)
TRAVEL = 512.0


def decoded(values):
    largest = jnp.max(jnp.abs(values), axis=-1, keepdims=True)
    largest = jnp.clip(largest, 2.0**-24, 2.0**8)
    stretched = largest * (2.0**23 + 1.0)
    lower = stretched - stretched * (1.0 - 2.0**-24)
    scaling = jnp.where(lower >= largest, lower, 2.0 * lower)
    step = scaling * (1.0 / 128.0)
    magic = scaling * (1.5 * 2.0**16)
    nearest = (values + magic) - magic
    half = scaling * (1.0 / 256.0)
    nearest = nearest + jnp.where(values - nearest >= half, step, 0.0)
    limit = scaling * (127.0 / 128.0)
    return jnp.clip(nearest, -limit, limit)


def encode_kernel(where, base, mine, other, out):
    for g in range(base.shape[-1] // GROUP):
        columns = pl.ds(g * GROUP, GROUP)
        start = base[0, :, columns].astype(jnp.float32)
        total = decoded(start - mine[0, :, columns].astype(jnp.float32))
        total += decoded(start - other[0, :, columns].astype(jnp.float32))
        out[0, :, columns] = total.astype(out.dtype)


def encode_pair(where, base, mine, other, count, dtype):
    rows, width = base.shape[1:]
    block = (1, rows, width)
    return pl.pallas_call(
        encode_kernel,
        grid_spec=pltpu.PrefetchScalarGridSpec(
            num_scalar_prefetch=1,
            grid=(count,),
            in_specs=[
                pl.BlockSpec(block, lambda i, w: (2 * w[i] + w[count], 0, 0)),
                pl.BlockSpec(block, lambda i, w: (2 * w[i] + w[count], 0, 0)),
                pl.BlockSpec(block, lambda i, w: (w[i], 0, 0)),
            ],
            out_specs=pl.BlockSpec(block, lambda i, w: (i, 0, 0)),
        ),
        out_shape=jax.ShapeDtypeStruct((count, rows, width), dtype),
        cost_estimate=pl.CostEstimate(
            flops=50 * count * rows * width, bytes_accessed=10 * count * rows * width, transcendentals=0
        ),
    )(where, base, mine, other)


def update_kernel(replicas, where, total, a, b, c, momentum, base, new_momentum, new_weights):
    for g in range(total.shape[-1] // GROUP):
        columns = pl.ds(g * GROUP, GROUP)
        near = a[0, :, columns].astype(jnp.float32) + b[0, :, columns].astype(jnp.float32)
        summed = total[0, :, columns] + (near + c[0, :, columns].astype(jnp.float32))
        average = summed / replicas
        moved = 0.9 * momentum[:, columns] + average
        new_momentum[:, columns] = moved
        outer = -0.7 * (average + 0.9 * moved)
        largest = jnp.max(jnp.abs(outer), axis=-1, keepdims=True) + EPSILON
        scaling = largest.astype(jnp.bfloat16).astype(jnp.float32)
        codes = (outer / scaling).astype(jnp.bfloat16).astype(jnp.float32)
        start = base[0, :, columns].astype(jnp.float32)
        new_weights[:, columns] = (start + codes * scaling).astype(jnp.bfloat16)


def update(where, replicas, total, a, b, c, momentum, base):
    rows, width = momentum.shape
    flat = pl.BlockSpec((rows, width), lambda i, w: (0, 0))
    first = pl.BlockSpec((1, rows, width), lambda i, w: (0, 0, 0))
    return pl.pallas_call(
        functools.partial(update_kernel, float(replicas)),
        grid_spec=pltpu.PrefetchScalarGridSpec(
            num_scalar_prefetch=1,
            grid=(1,),
            in_specs=[first] * 4 + [flat, pl.BlockSpec((1, rows, width), lambda i, w: (w[0], 0, 0))],
            out_specs=[flat, flat],
        ),
        out_shape=[
            jax.ShapeDtypeStruct((rows, width), jnp.float32),
            jax.ShapeDtypeStruct((rows, width), jnp.bfloat16),
        ],
    )(where, total, a, b, c, momentum, base)


def on_device(chips, local_weights, base_weights, momentum):
    rows, width = momentum.shape
    z, core = lax.axis_index("z"), lax.axis_index("core")

    def shift(values, by):
        pairs = [(2 * i + k, 2 * ((i + by) % chips) + k) for i in range(chips) for k in range(2)]
        return lax.ppermute(values, BOTH, pairs)

    def chips_at(offsets):
        return jnp.stack([lax.rem(z + k + chips, chips) for k in offsets] + [core]).astype(jnp.int32)

    mine = local_weights[0].reshape(2 * chips, rows, width)
    base = base_weights.reshape(2 * chips, rows, width)
    theirs = lax.dynamic_index_in_dim(mine.reshape(chips, 2, rows, width), 1 - core, 1, keepdims=False)
    swap = [(2 * i + k, 2 * i + 1 - k) for i in range(chips) for k in range(2)]
    other = lax.ppermute(theirs, BOTH, swap)

    right = shift(encode_pair(chips_at(RIGHT), base, mine, other, 4, jnp.bfloat16), 1)
    left = shift(encode_pair(chips_at(LEFT), base, mine, other, 4, jnp.bfloat16), -1)
    own = encode_pair(chips_at(OWN), base, mine, other, 4, jnp.float32)
    collected = own + (right.astype(jnp.float32) + left.astype(jnp.float32))
    sent = collected.astype(jnp.bfloat16)
    far = shift(sent[3:4], 6)
    a, b = shift(sent[1:2], 3), shift(sent[2:3], -3)

    where = (2 * z + core).astype(jnp.int32).reshape(1)
    new_momentum, mine_new = update(where, 2 * chips, collected[:1], a, b, far, momentum, base)
    travel = (mine_new.astype(jnp.float32) * TRAVEL).astype(jnp.float16)
    every = lax.all_gather(travel, BOTH, axis=0, tiled=True)
    new_weights = (every.astype(jnp.float32) * (1.0 / TRAVEL)).astype(jnp.bfloat16)
    return new_weights, new_momentum


def solution(mesh):
    fsdp, rep = mesh.devices.shape
    split = Mesh(mesh.devices.reshape(fsdp, rep // 2, 2), ("fsdp", "z", "core"))
    in_specs = (P(BOTH, "fsdp", None), P("fsdp", None), P(("fsdp",) + BOTH, None))
    out_specs = (P("fsdp", None), P(("fsdp",) + BOTH, None))
    return jax.shard_map(
        functools.partial(on_device, rep // 2), mesh=split, in_specs=in_specs, out_specs=out_specs, check_vma=False
    )
```

```python
import functools
import jax
import jax.numpy as jnp
from jax import lax
from jax.experimental import pallas as pl
from jax.experimental.pallas import tpu as pltpu
from jax.sharding import Mesh, PartitionSpec as P

EPSILON = 1e-06
GROUP = 128
BOTH = ("z", "core")
RIGHT = (1, 4, -2, 7)
LEFT = (-1, 2, -4, 5)
OWN = (0, 3, -3, 6)
OWN_CHIPS = len(OWN)
TRAVEL = 512.0
VMEM = 60 * 2**20


def decoded(values):
    largest = jnp.maximum(jnp.max(jnp.abs(values), axis=-1, keepdims=True), 2.0**-24)
    below = largest * (1.0 - 2.0**-24)
    stretched = below * (2.0**23 + 1.0)
    half = stretched - stretched * (1.0 - 2.0**-24)
    limit = half * (127.0 / 64.0)
    values = jnp.clip(values, -limit, limit)
    magic = half * (1.5 * 2.0**17)
    nearest = (values + magic) - magic
    return nearest + jnp.where(values - nearest >= half * (1.0 / 128.0), half * (1.0 / 64.0), 0.0)


def encode_kernel(chips, offsets, where, base, mine, other, *refs):
    outs, (base_in, mine_in, other_in, sems) = refs[:-4], refs[-4:]
    copies = []
    for i, offset in enumerate(offsets):
        chip = lax.rem(where[0] + (offset + chips), chips)
        row = 2 * chip + where[1]
        copies.append(
            [
                pltpu.make_async_copy(base.at[row], base_in.at[i], sems.at[i, 0]),
                pltpu.make_async_copy(mine.at[row], mine_in.at[i], sems.at[i, 1]),
                pltpu.make_async_copy(other.at[chip], other_in.at[i], sems.at[i, 2]),
            ]
        )
        for copy in copies[i]:
            copy.start()
    for i in range(len(offsets)):
        for copy in copies[i]:
            copy.wait()
        out = outs[i // OWN_CHIPS]
        for g in range(out.shape[-1] // GROUP):
            columns = pl.ds(g * GROUP, GROUP)
            start = base_in[i, :, columns].astype(jnp.float32)
            total = decoded(start - mine_in[i, :, columns].astype(jnp.float32))
            total += decoded(start - other_in[i, :, columns].astype(jnp.float32))
            out[i % OWN_CHIPS, :, columns] = total.astype(out.dtype)


def encode_pair(where, base, mine, other, offsets):
    rows, width = base.shape[1:]
    count = len(offsets)
    held = pltpu.VMEM((count, rows, width), jnp.bfloat16)
    kinds = count // OWN_CHIPS
    return pl.pallas_call(
        functools.partial(encode_kernel, base.shape[0] // 2, offsets),
        in_specs=[pl.BlockSpec(memory_space=pltpu.SMEM)] + [pl.BlockSpec(memory_space=pl.ANY)] * 3,
        out_specs=[pl.BlockSpec(memory_space=pltpu.VMEM)] * kinds,
        scratch_shapes=[held, held, held, pltpu.SemaphoreType.DMA((count, 3))],
        out_shape=[jax.ShapeDtypeStruct((OWN_CHIPS, rows, width), jnp.bfloat16)] * kinds,
        compiler_params=pltpu.CompilerParams(vmem_limit_bytes=VMEM),
        cost_estimate=pl.CostEstimate(
            flops=50 * count * rows * width, bytes_accessed=8 * count * rows * width, transcendentals=0
        ),
    )(where, base, mine, other)


def rounded(values):
    return lax.reduce_precision(values, exponent_bits=8, mantissa_bits=7)


def on_device(chips, local_weights, base_weights, momentum):
    rows, width = momentum.shape
    z, core = lax.axis_index("z"), lax.axis_index("core")

    def shift(values, by):
        pairs = [(2 * i + k, 2 * ((i + by) % chips) + k) for i in range(chips) for k in range(2)]
        return lax.ppermute(values, BOTH, pairs)

    where = jnp.stack([z, core]).astype(jnp.int32)
    mine = local_weights[0].reshape(2 * chips, rows, width)
    base = base_weights.reshape(2 * chips, rows, width)
    theirs = lax.dynamic_index_in_dim(mine.reshape(chips, 2, rows, width), 1 - core, 1, keepdims=False)
    swap = [(2 * i + k, 2 * i + 1 - k) for i in range(chips) for k in range(2)]
    other = lax.ppermute(theirs, BOTH, swap)

    to_right, to_left = encode_pair(where, base, mine, other, RIGHT + LEFT)
    right, left = shift(to_right, 1), shift(to_left, -1)
    (own,) = encode_pair(where, base, mine, other, OWN)

    def collected(i):
        parts = [part[i : i + 1].astype(jnp.float32) for part in (own, right, left)]
        return sum(parts).astype(jnp.bfloat16)

    farthest = collected(3)
    far = shift(farthest, 6)
    farthest, own, right, left = lax.optimization_barrier((farthest, own, right, left))
    up, down, total = shift(collected(1), 3), shift(collected(2), -3), collected(0)

    def wide(values):
        return values.reshape(rows, width).astype(jnp.float32)

    summed = wide(total) + (wide(up) + wide(down) + wide(far))
    average = summed / (2 * chips)
    new_momentum = 0.9 * momentum + average
    outer = -0.7 * (average + 0.9 * new_momentum)
    grouped = outer.reshape(rows, width // GROUP, GROUP)
    largest = jnp.max(jnp.abs(grouped), axis=-1) + EPSILON
    scaling = rounded(largest)[..., None]
    codes = rounded(grouped / scaling)
    row = lax.dynamic_index_in_dim(base, 2 * z + core, 0, keepdims=False).astype(jnp.float32)
    mine_new = rounded(row + (codes * scaling).reshape(rows, width))
    travel = (mine_new * TRAVEL).astype(jnp.float16)
    every = lax.all_gather(travel, BOTH, axis=0, tiled=True)
    new_weights = (every.astype(jnp.float32) * (1.0 / TRAVEL)).astype(jnp.bfloat16)
    return new_weights, new_momentum


def solution(mesh):
    fsdp, rep = mesh.devices.shape
    split = Mesh(mesh.devices.reshape(fsdp, rep // 2, 2), ("fsdp", "z", "core"))
    in_specs = (P(BOTH, "fsdp", None), P("fsdp", None), P(("fsdp",) + BOTH, None))
    out_specs = (P("fsdp", None), P(("fsdp",) + BOTH, None))
    return jax.shard_map(
        functools.partial(on_device, rep // 2), mesh=split, in_specs=in_specs, out_specs=out_specs, check_vma=False
    )
```
